32 devices in a mesh: bead: 2 (over y), atom: 4 (over z), ka: 4 (over x, core).
Axes of the slice: x: 2, y: 2, z: 4, core: 2. Of those that a mesh axis runs over, the one named last changes fastest.
Arguments:
- frac: float32 [3, 8192], P(None, ('bead', 'atom')), parts along dimension 1, may hold values from 0 to 1
- feat: bfloat16 [8192, 64], P(('bead', 'atom')), parts along dimension 0, may hold values from -6 to 6
- cotan: bfloat16 [8192, 64], P(('bead', 'atom')), parts along dimension 0, may hold values from -0.059814453 to 0.059814453
- kidx: int32 [3, 8192], P(None, 'ka'), may hold values from -12 to 12
- smear: float32 [64], replicated, may hold values from 0.001 to 0.01
Outputs:
- messages: float32 [8192, 64], P(('bead', 'atom')), parts along dimension 0
- forces: float32 [3, 8192], P(None, ('bead', 'atom')), parts along dimension 1
The draws below stay inside these ranges and needn't reach their ends.
There are 2 independent parts, one for each index of `bead`. The reference program is written for one: setup_inputs(seed, part) draws one part's arguments, and reference() takes and returns one part's arrays. A program takes and returns all parts, laid end to end along the dimension named above; an argument that names none is the same for every part. Nothing has to cross between parts.
All inputs are finite; a program needn't handle non-finite values.
Results may differ from the reference program's by a relative error of at most 0.0075.
Values may be sent and summed in bfloat16 or wider, within the bound.
A program may use at most 64 MiB of HBM per device.

```python
import math
import jax
import jax.numpy as jnp
from jax import lax

C = 64
KVEC = 8192
ATOM_DEV = 1024
ATOMS = 4096


def with_ends(drawn, rng, smallest, largest):
    index_at = [jax.random.randint(jax.random.fold_in(rng, axis), (), 0, length) for axis, length in enumerate(drawn.shape)]
    main_axis = drawn.shape.index(max(drawn.shape))
    neighbour = index_at[:main_axis] + [(index_at[main_axis] + 1) % drawn.shape[main_axis]] + index_at[main_axis + 1:]
    return drawn.at[tuple(index_at)].set(smallest).at[tuple(neighbour)].set(largest)


def shard_levels(own_key, shape, pieces, least, top_value):
    loudness = 1.0
    for axis_at, parts in pieces:
        steps = jax.random.uniform(jax.random.fold_in(jax.random.fold_in(own_key, 6), axis_at), (parts,), jnp.float32, least / len(pieces), top_value / len(pieces))
        loudness = loudness * jnp.repeat(jnp.exp(steps), shape[axis_at] // parts).reshape((-1,) + (1,) * (len(shape) - 1 - axis_at))
    return loudness


def bell_draw(key, dims, width, bound, shards=(), held_as=jnp.bfloat16):
    entries = width * jax.random.normal(key, dims, jnp.float32)
    if shards:
        entries = entries * shard_levels(key, dims, shards, -0.22, 0.18)
    return jnp.clip(entries, -bound, bound).astype(held_as)


def setup_inputs(seed: int = 0, part: int = 0) -> dict:
    streams_of = jax.random.split(jax.random.key(seed), 6)
    part_splits = jax.random.split(jax.random.fold_in(streams_of[5], part), 6)
    return {
        "frac": jnp.clip(1.0 * jax.random.uniform(part_splits[0], (3, ATOMS), jnp.float32) ** shard_levels(part_splits[0], (3, ATOMS), ((1, 4),), -0.2, 0.2), 0.0, 1.0),
        "feat": bell_draw(part_splits[1], (ATOMS, C), 1.0, 6.0, ((0, 4),)),
        "cotan": bell_draw(part_splits[2], (ATOMS, C), 0.01, 0.059814453, ((0, 4),)),
        "kidx": with_ends(jax.random.randint(streams_of[3], (3, KVEC), -12, 13), jax.random.fold_in(streams_of[3], 1), -12, 12).astype(jnp.int32),
        "smear": jnp.clip(jnp.exp(jax.random.uniform(streams_of[4], (C,), jnp.float32, math.log(0.001), math.log(0.01))), 0.001, 0.01),
    }


TWO_PI = 2.0 * math.pi


def phases(frac_block, nf):
    spot = frac_block[0][:, None] * nf[0][None, :] + frac_block[1][:, None] * nf[1][None, :]
    spot = spot + frac_block[2][:, None] * nf[2][None, :]
    theta = TWO_PI * spot
    return jnp.cos(theta).astype(jnp.bfloat16), jnp.sin(theta).astype(jnp.bfloat16)


def over_rows(table, columns):
    return lax.dot_general(table, columns, (((0,), (0,)), ((), ())), preferred_element_type=jnp.float32)


def against(left, right):
    return lax.dot_general(left, right, (((1,), (1,)), ((), ())), preferred_element_type=jnp.float32)


def reference(frac, feat, cotan, kidx, smear):
    nf = kidx.astype(jnp.float32)
    nsq = nf[0] * nf[0] + nf[1] * nf[1] + nf[2] * nf[2]
    weights = jnp.exp(-smear[None, :] * nsq[:, None]) / (1.0 + nsq)[:, None] * (ATOMS ** -0.5)
    block = ATOM_DEV if ATOM_DEV <= 1024 else 1024
    count = ATOMS // block
    fblocks = frac.reshape(3, count, block).transpose(1, 0, 2)
    feat_blocks = feat.reshape(count, block, C)
    cot_blocks = cotan.reshape(count, block, C)

    def accumulate(total, items):
        fpiece, hpiece, apiece = items
        cos_t, sin_t = phases(fpiece, nf)
        both = jnp.concatenate([hpiece, apiece], axis=1)
        return total + jnp.concatenate([over_rows(cos_t, both), over_rows(sin_t, both)], axis=1), None

    total, unused = lax.scan(accumulate, jnp.zeros((KVEC, 4 * C), jnp.float32), (fblocks, feat_blocks, cot_blocks))
    weighted = (total * jnp.tile(weights, (1, 4))).astype(jnp.bfloat16)
    left_c = weighted[:, :2 * C]
    left_s = weighted[:, 2 * C:]
    nbf = kidx.astype(jnp.bfloat16)

    def outputs(items):
        fpiece, hpiece, apiece = items
        cos_t, sin_t = phases(fpiece, nf)
        msg = jnp.dot(cos_t, left_c[:, :C], preferred_element_type=jnp.float32) + jnp.dot(sin_t, left_s[:, :C], preferred_element_type=jnp.float32)
        pair = jnp.concatenate([apiece, hpiece], axis=1)
        p_part = against(pair, left_c)
        q_part = against(pair, left_s)
        slope = (cos_t.astype(jnp.float32) * q_part - sin_t.astype(jnp.float32) * p_part).astype(jnp.bfloat16)
        force = -TWO_PI * against(nbf, slope)
        return msg, force

    msgs, force_blocks = lax.map(outputs, (fblocks, feat_blocks, cot_blocks))
    messages = msgs.reshape(ATOMS, C)
    forces = force_blocks.transpose(1, 0, 2).reshape(3, ATOMS)
    return messages, forces
```

```python
import functools
import math

import jax
import jax.numpy as jnp
import numpy as np
from jax import lax
from jax.experimental import pallas as pl
from jax.experimental.pallas import tpu as pltpu
from jax.sharding import PartitionSpec as P

TWO_PI = 2.0 * math.pi
MESH = pl.DeviceIdType.MESH
F32 = jnp.float32
BF16 = jnp.bfloat16
ROUND = 1.5 * 2.0**23


def half_turn_fit():
    nodes = 0.125 * (1.0 - np.cos(np.pi * (np.arange(400) + 0.5) / 400))
    t = np.sqrt(nodes)
    root = math.sqrt(2.0)
    sin_c = np.polynomial.chebyshev.Chebyshev.fit(nodes, root * np.sin(np.pi * t) / t, 3, domain=[0, 0.25])
    cos_c = np.polynomial.chebyshev.Chebyshev.fit(nodes, root * np.cos(np.pi * t), 3, domain=[0, 0.25])
    to_list = lambda fit: [float(v) for v in fit.convert(kind=np.polynomial.Polynomial, domain=[-1, 1]).coef]
    return to_list(sin_c), to_list(cos_c)


SIN_C, COS_C = half_turn_fit()


def turn(spot):
    t = spot - ((spot + ROUND) - ROUND)
    u = t * t
    half_s = t * (((SIN_C[3] * u + SIN_C[2]) * u + SIN_C[1]) * u + SIN_C[0])
    half_c = ((COS_C[3] * u + COS_C[2]) * u + COS_C[1]) * u + COS_C[0]
    return (1.0 - half_s * half_s).astype(BF16), (half_s * half_c).astype(BF16)


def kernel(
    atoms, frac_ref, feat_ref, cot_ref, kidx_ref, smear_ref, msg_ref, force_ref,
    fr, fs, xt, ph, gt, part, rc, s1, rx, s2, rz, fin,
    fsend, frecv, zsend, zrecv, xsend, xrecv, csend, crecv,
    pcs, pcr, pxs, pxr, pzs, pzr, ags, agr,
):
    bead = lax.axis_index("bead")
    z = lax.axis_index("atom")
    ka = lax.axis_index("ka")
    x = ka // 2
    core = lax.rem(ka, 2)
    slot = core * 2 + x
    other_core = 1 - core
    dev_z = [(bead, lax.rem(z + j, 4), ka) for j in range(4)]
    dev_core = (bead, z, x * 2 + other_core)
    dev_x = (bead, z, (1 - x) * 2 + core)
    dev_diag = (bead, z, (1 - x) * 2 + other_core)
    kn = kidx_ref.shape[1] // 4
    quarter = fr.shape[2] // 4

    barrier = pltpu.get_barrier_semaphore()
    for dev in dev_z[1:] + [dev_core, dev_x, dev_diag]:
        pl.semaphore_signal(barrier, inc=1, device_id=dev, device_id_type=MESH)

    def remote(src, dst, send, recv, dev):
        return pltpu.make_async_remote_copy(
            src_ref=src, dst_ref=dst, send_sem=send, recv_sem=recv, device_id=dev, device_id_type=MESH
        )

    fr[0] = jnp.zeros(fr.shape[1:], F32)
    fr[0, 0:3, :] = frac_ref[...]
    for s in range(4):
        rows = pl.ds(s * quarter, quarter)
        both = jnp.concatenate([feat_ref[rows, :].astype(F32), cot_ref[rows, :].astype(F32)], axis=1)
        xt[0, s] = both.T.astype(BF16)

    pl.semaphore_wait(barrier, 6)
    fcopies = [remote(fr.at[0], fr.at[4 - j], fsend.at[j], frecv.at[4 - j], dev_z[j]) for j in (1, 3, 2)]
    for c in fcopies:
        c.start()
    zcopies = [
        remote(xt.at[0, slot], xt.at[4 - j, slot], zsend.at[j], zrecv.at[4 - j], dev_z[j]) for j in (1, 3, 2)
    ]
    for c in zcopies:
        c.start()

    kf = kidx_ref[:, pl.ds(pl.multiple_of(z * kn, 128), kn)].astype(F32)
    k0, k1, k2 = kf[0:1], kf[1:2], kf[2:3]
    row = lax.broadcasted_iota(jnp.int32, (8, kn), 0)
    k8 = jnp.where(row == 0, k0, jnp.where(row == 1, k1, jnp.where(row == 2, k2, 0.0)))
    kt = jnp.concatenate([k8, k8, k8, jnp.zeros((104, kn), F32)], axis=0).T.astype(BF16)[:, :32]

    def phases(r):
        f = fr[r]
        hi = f.astype(BF16).astype(F32)
        mid = (f - hi).astype(BF16).astype(F32)
        lo = f - hi - mid
        fs[...] = jnp.concatenate([hi, mid, lo, jnp.zeros_like(f)], axis=0).astype(BF16)
        for s in range(4):
            spot = jnp.dot(kt, fs[:, s * quarter : (s + 1) * quarter], preferred_element_type=F32)
            c, sn = turn(spot)
            ph[r, s, 0:kn, :] = c
            ph[r, s, kn : 2 * kn, :] = sn

    def sums_of(r):
        total = None
        for s in range(4):
            term = lax.dot_general(
                ph[r, s], xt[r, s], (((1,), (1,)), ((), ())), preferred_element_type=F32
            )
            total = term if total is None else total + term
        return total

    def wait_frac(r):
        remote(fr.at[0], fr.at[r], fsend.at[0], frecv.at[r], dev_x).wait_recv()

    phases(0)
    xcopies = []
    for r in (1, 3, 2):
        remote(xt.at[0, slot], xt.at[r, slot], zsend.at[0], zrecv.at[r], dev_x).wait_recv()
        c = remote(xt.at[r, slot], xt.at[r, slot], xsend.at[r], xrecv.at[r], dev_x)
        c.start()
        xcopies.append(c)
    wait_frac(1)
    phases(1)
    ccopies = []
    mate = core * 2 + (1 - x)
    two = pl.ds(core * 2, 2)
    for r in (1, 3, 2):
        remote(xt.at[r, mate], xt.at[r, mate], xsend.at[r], xrecv.at[r], dev_x).wait_recv()
        c = remote(xt.at[r, two], xt.at[r, two], csend.at[r], crecv.at[r], dev_core)
        c.start()
        ccopies.append(c)
    wait_frac(3)
    phases(3)
    wait_frac(2)
    phases(2)

    total = sums_of(0)
    other_two = pl.ds(other_core * 2, 2)
    for r in (1, 3, 2):
        remote(xt.at[r, other_two], xt.at[r, other_two], csend.at[r], crecv.at[r], dev_core).wait_recv()
        total = total + sums_of(r)
    sums_t = total.T

    nsq = k0 * k0 + k1 * k1 + k2 * k2
    srow = jnp.concatenate([smear_ref[...], smear_ref[...]], axis=1)
    scol = jnp.broadcast_to(srow, (128, 128)).T
    scol = jnp.concatenate([scol] * (kn // 128), axis=1)
    weights = jnp.exp(-scol * nsq) / (1.0 + nsq) * atoms ** (-0.5)
    wc = (sums_t[:, :kn] * weights).astype(BF16)
    ws = (sums_t[:, kn:] * weights).astype(BF16)
    half = wc.shape[0] // 2
    gt[384:448, 0:kn] = wc[:half]
    gt[384:448, kn : 2 * kn] = ws[:half]
    wc, ws = wc.astype(F32), ws.astype(F32)
    wc = jnp.concatenate([wc[half:], wc[:half]], axis=0)
    ws = jnp.concatenate([ws[half:], ws[:half]], axis=0)
    for d, kd in enumerate((k0, k1, k2)):
        gt[128 * d : 128 * d + 128, 0:kn] = (ws * kd).astype(BF16)
        gt[128 * d : 128 * d + 128, kn : 2 * kn] = (wc * -kd).astype(BF16)

    frow = lax.broadcasted_iota(jnp.int32, (16, quarter), 0)

    def outputs_of(r, i):
        for s in range(4):
            out = jnp.dot(gt[...], ph[r, s], preferred_element_type=F32)
            pair = xt[r, s].astype(F32)
            f = [
                -TWO_PI * jnp.sum(out[128 * d : 128 * d + 128] * pair, axis=0, keepdims=True) for d in range(3)
            ]
            part[i, s, 0:64, :] = out[384:448].astype(BF16)
            part[i, s, 64:80, :] = jnp.where(
                frow == 0, f[0], jnp.where(frow == 1, f[1], jnp.where(frow == 2, f[2], 0.0))
            ).astype(BF16)

    pending = []

    def begin(c):
        c.start()
        pending.append(c)

    own = None
    for i in range(6):
        if i < 4:
            outputs_of((1 + i) % 4, i)
            begin(remote(part.at[i, other_two], rc.at[i], pcs.at[i], pcr.at[i], dev_core))
        if 1 <= i < 5:
            j = i - 1
            remote(part.at[j, two], rc.at[j], pcs.at[j], pcr.at[j], dev_core).wait_recv()
            s1[j] = (part[j, two].astype(F32) + rc[j].astype(F32)).astype(BF16)
            begin(remote(s1.at[j, 1 - x], rx.at[j], pxs.at[j], pxr.at[j], dev_x))
        if i >= 2:
            j = i - 2
            remote(s1.at[j, x], rx.at[j], pxs.at[j], pxr.at[j], dev_x).wait_recv()
            value = s1[j, x].astype(F32) + rx[j].astype(F32)
            if j < 3:
                s2[j] = value.astype(BF16)
                begin(remote(s2.at[j], rz.at[j], pzs.at[j], pzr.at[j], dev_z[1 + j]))
            else:
                own = value
    for j in range(3):
        remote(s2.at[j], rz.at[j], pzs.at[j], pzr.at[j], dev_x).wait_recv()
        own = own + rz[j].astype(F32)
    fin[slot] = own.astype(BF16)
    for j, dev in enumerate((dev_x, dev_core, dev_diag)):
        begin(remote(fin.at[slot], fin.at[slot], ags.at[j], agr.at[j], dev))
    slots = (mate, other_core * 2 + x, other_core * 2 + (1 - x))
    for j, dev in enumerate((dev_x, dev_core, dev_diag)):
        remote(fin.at[slots[j]], fin.at[slots[j]], ags.at[j], agr.at[j], dev).wait_recv()
    for s in range(4):
        msg_ref[s * quarter : (s + 1) * quarter, :] = fin[s, 0:64, :].astype(F32).T
        force_ref[:, s * quarter : (s + 1) * quarter] = fin[s, 64:80, :].astype(F32)[0:3]
    for c in fcopies + zcopies + xcopies + ccopies + pending:
        c.wait_send()


def fast_on_device(frac, feat, cotan, kidx, smear):
    rows, chans = feat.shape
    kn = kidx.shape[1] // 4
    quarter = rows // 4
    dma = pltpu.SemaphoreType.DMA
    vmem = pl.BlockSpec(memory_space=pltpu.VMEM)
    return pl.pallas_call(
        functools.partial(kernel, 4 * rows),
        out_shape=(jax.ShapeDtypeStruct((rows, chans), F32), jax.ShapeDtypeStruct((3, rows), F32)),
        in_specs=[vmem] * 5,
        out_specs=(vmem, vmem),
        scratch_shapes=[
            pltpu.VMEM((4, 8, rows), F32),
            pltpu.VMEM((32, rows), BF16),
            pltpu.VMEM((4, 4, 128, quarter), BF16),
            pltpu.VMEM((4, 4, 2 * kn, quarter), BF16),
            pltpu.VMEM((448, 2 * kn), BF16),
            pltpu.VMEM((4, 4, 80, quarter), BF16),
            pltpu.VMEM((4, 2, 80, quarter), BF16),
            pltpu.VMEM((4, 2, 80, quarter), BF16),
            pltpu.VMEM((4, 80, quarter), BF16),
            pltpu.VMEM((3, 80, quarter), BF16),
            pltpu.VMEM((3, 80, quarter), BF16),
            pltpu.VMEM((4, 80, quarter), BF16),
        ]
        + [dma((4,))] * 16,
        compiler_params=pltpu.CompilerParams(
            collective_id=0, has_side_effects=True, vmem_limit_bytes=48 * 1024 * 1024
        ),
    )(frac, feat, cotan, kidx, smear.reshape(1, chans))


def over_rows(table, columns):
    return lax.dot_general(table, columns, (((0,), (0,)), ((), ())), preferred_element_type=F32)


def plain_on_device(frac, feat, cotan, kidx, smear):
    rows, chans = feat.shape
    atoms = rows * lax.axis_size("atom")
    nf = kidx.astype(F32)
    nsq = nf[0] * nf[0] + nf[1] * nf[1] + nf[2] * nf[2]
    weights = jnp.exp(-smear[None, :] * nsq[:, None]) / (1.0 + nsq)[:, None] * atoms ** (-0.5)
    spot = frac[0][:, None] * nf[0][None, :] + frac[1][:, None] * nf[1][None, :]
    cos_t, sin_t = turn(spot + frac[2][:, None] * nf[2][None, :])
    both = jnp.concatenate([feat, cotan], axis=1)
    sums = jnp.concatenate([over_rows(cos_t, both), over_rows(sin_t, both)], axis=1)
    total = lax.psum(sums, "atom")
    weighted = (total * jnp.tile(weights, (1, 4))).astype(BF16)
    left_c, left_s = weighted[:, : 2 * chans], weighted[:, 2 * chans :]
    msg = jnp.dot(cos_t, left_c[:, :chans], preferred_element_type=F32)
    msg = msg + jnp.dot(sin_t, left_s[:, :chans], preferred_element_type=F32)
    pair = jnp.concatenate([cotan, feat], axis=1)
    against = lambda a, b: lax.dot_general(a, b, (((1,), (1,)), ((), ())), preferred_element_type=F32)
    p_part, q_part = against(pair, left_c), against(pair, left_s)
    slope = (cos_t.astype(F32) * q_part - sin_t.astype(F32) * p_part).astype(BF16)
    force = -TWO_PI * against(kidx.astype(BF16), slope)
    return lax.psum(msg, "ka"), lax.psum(force, "ka")


def on_device(frac, feat, cotan, kidx, smear):
    rows, chans = feat.shape
    fits = lax.axis_size("atom") == 4 and lax.axis_size("ka") == 4 and chans == 64
    fits = fits and rows % 512 == 0 and rows <= 1024 and kidx.shape[1] % 512 == 0 and kidx.shape[1] <= 2048
    return (fast_on_device if fits else plain_on_device)(frac, feat, cotan, kidx, smear)


def solution(mesh):
    return jax.shard_map(
        on_device,
        mesh=mesh,
        in_specs=(
            P(None, ("bead", "atom")),
            P(("bead", "atom"), None),
            P(("bead", "atom"), None),
            P(None, "ka"),
            P(),
        ),
        out_specs=(P(("bead", "atom"), None), P(None, ("bead", "atom"))),
        check_vma=False,
    )
```

```python
import functools
import math

import jax
import jax.numpy as jnp
import numpy as np
from jax import lax
from jax.experimental import pallas as pl
from jax.experimental.pallas import tpu as pltpu
from jax.sharding import PartitionSpec as P

TWO_PI = 2.0 * math.pi
MESH = pl.DeviceIdType.MESH
F32 = jnp.float32
BF16 = jnp.bfloat16
ROUND = 1.5 * 2.0**23


def half_turn_fit():
    nodes = 0.125 * (1.0 - np.cos(np.pi * (np.arange(400) + 0.5) / 400))
    t = np.sqrt(nodes)
    root = math.sqrt(2.0)
    sin_c = np.polynomial.chebyshev.Chebyshev.fit(nodes, root * np.sin(np.pi * t) / t, 3, domain=[0, 0.25])
    cos_c = np.polynomial.chebyshev.Chebyshev.fit(nodes, root * np.cos(np.pi * t), 3, domain=[0, 0.25])
    to_list = lambda fit: [float(v) for v in fit.convert(kind=np.polynomial.Polynomial, domain=[-1, 1]).coef]
    return to_list(sin_c), to_list(cos_c)


SIN_C, COS_C = half_turn_fit()


def turn(spot):
    t = spot - ((spot + ROUND) - ROUND)
    u = t * t
    half_s = t * (((SIN_C[3] * u + SIN_C[2]) * u + SIN_C[1]) * u + SIN_C[0])
    half_c = ((COS_C[3] * u + COS_C[2]) * u + COS_C[1]) * u + COS_C[0]
    return (1.0 - half_s * half_s).astype(BF16), (half_s * half_c).astype(BF16)


def kernel(
    atoms, frac_hbm, feat_hbm, cot_hbm, kidx_hbm, smear_hbm, msg_ref, force_ref,
    frac_ref, feat_ref, cot_ref, kidx_ref, smear_ref, lsem,
    fr, f8, fs, xt, ph, gt, part, rc, s1, rx, s2, rz, fin,
    fsend, frecv, zsend, zrecv, xsend, xrecv, csend, crecv,
    pcs, pcr, pxs, pxr, pzs, pzr, ags, agr,
):
    bead = lax.axis_index("bead")
    z = lax.axis_index("atom")
    ka = lax.axis_index("ka")
    x = ka // 2
    core = lax.rem(ka, 2)
    slot = core * 2 + x
    other_core = 1 - core
    dev_z = [(bead, lax.rem(z + j, 4), ka) for j in range(4)]
    dev_core = (bead, z, x * 2 + other_core)
    dev_x = (bead, z, (1 - x) * 2 + core)
    dev_diag = (bead, z, (1 - x) * 2 + other_core)
    kn = kidx_ref.shape[1]
    quarter = fr.shape[2] // 4

    barrier = pltpu.get_barrier_semaphore()
    for dev in dev_z[1:] + [dev_core, dev_x, dev_diag]:
        pl.semaphore_signal(barrier, inc=1, device_id=dev, device_id_type=MESH)

    def remote(src, dst, send, recv, dev):
        return pltpu.make_async_remote_copy(
            src_ref=src, dst_ref=dst, send_sem=send, recv_sem=recv, device_id=dev, device_id_type=MESH
        )

    loads = [
        pltpu.make_async_copy(frac_hbm, frac_ref, lsem.at[0]),
        pltpu.make_async_copy(feat_hbm, feat_ref, lsem.at[1]),
        pltpu.make_async_copy(cot_hbm, cot_ref, lsem.at[2]),
        pltpu.make_async_copy(kidx_hbm.at[:, pl.ds(pl.multiple_of(z * kn, 128), kn)], kidx_ref, lsem.at[3]),
        pltpu.make_async_copy(smear_hbm, smear_ref, lsem.at[4]),
    ]
    for c in loads:
        c.start()
    f8[...] = jnp.zeros(f8.shape, F32)
    loads[0].wait()
    fr[0] = frac_ref[...]
    loads[1].wait()
    loads[2].wait()
    for s in range(4):
        cols = pl.ds(s * quarter, quarter)
        xt[0, s, 0:64, :] = feat_ref[:, cols]
        xt[0, s, 64:128, :] = cot_ref[:, cols]

    pl.semaphore_wait(barrier, 6)
    fcopies = [remote(fr.at[0], fr.at[4 - j], fsend.at[j], frecv.at[4 - j], dev_z[j]) for j in (1, 3, 2)]
    for c in fcopies:
        c.start()
    zcopies = [
        remote(xt.at[0, slot], xt.at[4 - j, slot], zsend.at[j], zrecv.at[4 - j], dev_z[j]) for j in (1, 3, 2)
    ]
    for c in zcopies:
        c.start()

    loads[3].wait()
    loads[4].wait()
    kf = kidx_ref[...].astype(F32)
    k0, k1, k2 = kf[0:1], kf[1:2], kf[2:3]
    row = lax.broadcasted_iota(jnp.int32, (8, kn), 0)
    k8 = jnp.where(row == 0, k0, jnp.where(row == 1, k1, jnp.where(row == 2, k2, 0.0)))
    kt = jnp.concatenate([k8, k8, k8, jnp.zeros((104, kn), F32)], axis=0).T.astype(BF16)[:, :32]

    def phases(r):
        f8[0:3, :] = fr[r]
        f = f8[...]
        hi = f.astype(BF16).astype(F32)
        mid = (f - hi).astype(BF16).astype(F32)
        lo = f - hi - mid
        fs[...] = jnp.concatenate([hi, mid, lo, jnp.zeros_like(f)], axis=0).astype(BF16)
        for s in range(4):
            spot = jnp.dot(kt, fs[:, s * quarter : (s + 1) * quarter], preferred_element_type=F32)
            c, sn = turn(spot)
            ph[r, s, 0:kn, :] = c
            ph[r, s, kn : 2 * kn, :] = sn

    def sums_of(r):
        total = None
        for s in range(4):
            term = lax.dot_general(
                ph[r, s], xt[r, s], (((1,), (1,)), ((), ())), preferred_element_type=F32
            )
            total = term if total is None else total + term
        return total

    def wait_frac(r):
        remote(fr.at[0], fr.at[r], fsend.at[0], frecv.at[r], dev_x).wait_recv()

    nsq = k0 * k0 + k1 * k1 + k2 * k2
    srow = jnp.concatenate([smear_ref[...], smear_ref[...]], axis=1)
    scol = jnp.broadcast_to(srow, (128, 128)).T
    scol = jnp.concatenate([scol] * (kn // 128), axis=1)
    weights = jnp.exp(-scol * nsq) / (1.0 + nsq) * atoms ** (-0.5)
    mate = core * 2 + (1 - x)
    two = pl.ds(core * 2, 2)
    other_two = pl.ds(other_core * 2, 2)
    xcopies, ccopies = [], []

    def forward_x(r):
        remote(xt.at[0, slot], xt.at[r, slot], zsend.at[0], zrecv.at[r], dev_x).wait_recv()
        xcopies.append(remote(xt.at[r, slot], xt.at[r, slot], xsend.at[r], xrecv.at[r], dev_x))
        xcopies[-1].start()

    def forward_core(r):
        remote(xt.at[r, mate], xt.at[r, mate], xsend.at[r], xrecv.at[r], dev_x).wait_recv()
        ccopies.append(remote(xt.at[r, two], xt.at[r, two], csend.at[r], crecv.at[r], dev_core))
        ccopies[-1].start()

    def wait_core(r):
        remote(xt.at[r, other_two], xt.at[r, other_two], csend.at[r], crecv.at[r], dev_core).wait_recv()

    phases(0)
    wait_frac(1)
    phases(1)
    forward_x(1)
    forward_x(3)
    total = sums_of(0)
    forward_core(1)
    forward_x(2)
    wait_frac(3)
    phases(3)
    forward_core(3)
    wait_core(1)
    total = total + sums_of(1)
    forward_core(2)
    wait_frac(2)
    phases(2)
    wait_core(3)
    total = total + sums_of(3)
    wait_core(2)
    total = total + sums_of(2)
    sums_t = total.T

    wc = (sums_t[:, :kn] * weights).astype(BF16)
    ws = (sums_t[:, kn:] * weights).astype(BF16)
    half = wc.shape[0] // 2
    gt[384:448, 0:kn] = wc[:half]
    gt[384:448, kn : 2 * kn] = ws[:half]
    wc, ws = wc.astype(F32), ws.astype(F32)
    wc = jnp.concatenate([wc[half:], wc[:half]], axis=0)
    ws = jnp.concatenate([ws[half:], ws[:half]], axis=0)
    for d, kd in enumerate((k0, k1, k2)):
        gt[128 * d : 128 * d + 128, 0:kn] = (ws * kd).astype(BF16)
        gt[128 * d : 128 * d + 128, kn : 2 * kn] = (wc * -kd).astype(BF16)

    frow = lax.broadcasted_iota(jnp.int32, (16, quarter), 0)

    def outputs_of(r, i, slots):
        for s in slots:
            out = jnp.dot(gt[...], ph[r, s], preferred_element_type=F32)
            pair = xt[r, s].astype(F32)
            f = [
                -TWO_PI * jnp.sum(out[128 * d : 128 * d + 128] * pair, axis=0, keepdims=True) for d in range(3)
            ]
            part[i, s, 0:64, :] = out[384:448].astype(BF16)
            part[i, s, 64:80, :] = jnp.where(
                frow == 0, f[0], jnp.where(frow == 1, f[1], jnp.where(frow == 2, f[2], 0.0))
            ).astype(BF16)

    pending = []

    def begin(c):
        c.start()
        pending.append(c)

    for i in range(4):
        outputs_of((1 + i) % 4, i, (other_core * 2, other_core * 2 + 1))
        begin(remote(part.at[i, other_two], rc.at[i], pcs.at[i], pcr.at[i], dev_core))
    for i in range(4):
        outputs_of((1 + i) % 4, i, (mate,))
        remote(part.at[i, two], rc.at[i], pcs.at[i], pcr.at[i], dev_core).wait_recv()
        s1[i] = (part[i, mate].astype(F32) + rc[i, 1 - x].astype(F32)).astype(BF16)
        begin(remote(s1.at[i], rx.at[i], pxs.at[i], pxr.at[i], dev_x))
    own = None
    for i in range(4):
        outputs_of((1 + i) % 4, i, (slot,))
        remote(s1.at[i], rx.at[i], pxs.at[i], pxr.at[i], dev_x).wait_recv()
        own = part[i, slot].astype(F32) + rc[i, x].astype(F32) + rx[i].astype(F32)
        if i < 3:
            s2[i] = own.astype(BF16)
            begin(remote(s2.at[i], rz.at[i], pzs.at[i], pzr.at[i], dev_z[1 + i]))
    for j in range(3):
        remote(s2.at[j], rz.at[j], pzs.at[j], pzr.at[j], dev_x).wait_recv()
        own = own + rz[j].astype(F32)
    fin[slot] = own.astype(BF16)
    for j, dev in enumerate((dev_x, dev_core, dev_diag)):
        begin(remote(fin.at[slot], fin.at[slot], ags.at[j], agr.at[j], dev))
    slots = (mate, other_core * 2 + x, other_core * 2 + (1 - x))
    for j, dev in enumerate((dev_x, dev_core, dev_diag)):
        remote(fin.at[slots[j]], fin.at[slots[j]], ags.at[j], agr.at[j], dev).wait_recv()
    for s in range(4):
        msg_ref[:, s * quarter : (s + 1) * quarter] = fin[s, 0:64, :].astype(F32)
        force_ref[:, s * quarter : (s + 1) * quarter] = fin[s, 64:80, :].astype(F32)[0:3]
    for c in fcopies + zcopies + xcopies + ccopies + pending:
        c.wait_send()


def fast_on_device(frac, feat, cotan, kidx, smear):
    rows, chans = feat.shape
    kn = kidx.shape[1] // 4
    quarter = rows // 4
    dma = pltpu.SemaphoreType.DMA
    vmem = pl.BlockSpec(memory_space=pltpu.VMEM)
    messages_t, forces = pl.pallas_call(
        functools.partial(kernel, 4 * rows),
        out_shape=(jax.ShapeDtypeStruct((chans, rows), F32), jax.ShapeDtypeStruct((3, rows), F32)),
        in_specs=[pl.BlockSpec(memory_space=pl.ANY)] * 5,
        out_specs=(vmem, vmem),
        scratch_shapes=[
            pltpu.VMEM((3, rows), F32),
            pltpu.VMEM((chans, rows), BF16),
            pltpu.VMEM((chans, rows), BF16),
            pltpu.VMEM((3, kn), jnp.int32),
            pltpu.VMEM((1, chans), F32),
            dma((5,)),
            pltpu.VMEM((4, 3, rows), F32),
            pltpu.VMEM((8, rows), F32),
            pltpu.VMEM((32, rows), BF16),
            pltpu.VMEM((4, 4, 128, quarter), BF16),
            pltpu.VMEM((4, 4, 2 * kn, quarter), BF16),
            pltpu.VMEM((448, 2 * kn), BF16),
            pltpu.VMEM((4, 4, 80, quarter), BF16),
            pltpu.VMEM((4, 2, 80, quarter), BF16),
            pltpu.VMEM((4, 80, quarter), BF16),
            pltpu.VMEM((4, 80, quarter), BF16),
            pltpu.VMEM((3, 80, quarter), BF16),
            pltpu.VMEM((3, 80, quarter), BF16),
            pltpu.VMEM((4, 80, quarter), BF16),
        ]
        + [dma((4,))] * 16,
        compiler_params=pltpu.CompilerParams(
            collective_id=0, has_side_effects=True, vmem_limit_bytes=48 * 1024 * 1024
        ),
    )(frac, feat.T, cotan.T, kidx, smear.reshape(1, chans))
    return messages_t.T, forces


def over_rows(table, columns):
    return lax.dot_general(table, columns, (((0,), (0,)), ((), ())), preferred_element_type=F32)


def plain_on_device(frac, feat, cotan, kidx, smear):
    rows, chans = feat.shape
    atoms = rows * lax.axis_size("atom")
    nf = kidx.astype(F32)
    nsq = nf[0] * nf[0] + nf[1] * nf[1] + nf[2] * nf[2]
    weights = jnp.exp(-smear[None, :] * nsq[:, None]) / (1.0 + nsq)[:, None] * atoms ** (-0.5)
    spot = frac[0][:, None] * nf[0][None, :] + frac[1][:, None] * nf[1][None, :]
    cos_t, sin_t = turn(spot + frac[2][:, None] * nf[2][None, :])
    both = jnp.concatenate([feat, cotan], axis=1)
    sums = jnp.concatenate([over_rows(cos_t, both), over_rows(sin_t, both)], axis=1)
    total = lax.psum(sums, "atom")
    weighted = (total * jnp.tile(weights, (1, 4))).astype(BF16)
    left_c, left_s = weighted[:, : 2 * chans], weighted[:, 2 * chans :]
    msg = jnp.dot(cos_t, left_c[:, :chans], preferred_element_type=F32)
    msg = msg + jnp.dot(sin_t, left_s[:, :chans], preferred_element_type=F32)
    pair = jnp.concatenate([cotan, feat], axis=1)
    against = lambda a, b: lax.dot_general(a, b, (((1,), (1,)), ((), ())), preferred_element_type=F32)
    p_part, q_part = against(pair, left_c), against(pair, left_s)
    slope = (cos_t.astype(F32) * q_part - sin_t.astype(F32) * p_part).astype(BF16)
    force = -TWO_PI * against(kidx.astype(BF16), slope)
    return lax.psum(msg, "ka"), lax.psum(force, "ka")


def on_device(frac, feat, cotan, kidx, smear):
    rows, chans = feat.shape
    fits = lax.axis_size("atom") == 4 and lax.axis_size("ka") == 4 and chans == 64
    fits = fits and rows % 512 == 0 and rows <= 1024 and kidx.shape[1] % 512 == 0 and kidx.shape[1] <= 2048
    return (fast_on_device if fits else plain_on_device)(frac, feat, cotan, kidx, smear)


def solution(mesh):
    return jax.shard_map(
        on_device,
        mesh=mesh,
        in_specs=(
            P(None, ("bead", "atom")),
            P(("bead", "atom"), None),
            P(("bead", "atom"), None),
            P(None, "ka"),
            P(),
        ),
        out_specs=(P(("bead", "atom"), None), P(None, ("bead", "atom"))),
        check_vma=False,
    )
```

```python
import functools
import math

import jax
import jax.numpy as jnp
import numpy as np
from jax import lax
from jax.experimental import pallas as pl
from jax.experimental.pallas import tpu as pltpu
from jax.sharding import PartitionSpec as P

TWO_PI = 2.0 * math.pi
MESH = pl.DeviceIdType.MESH
F32 = jnp.float32
BF16 = jnp.bfloat16
ROUND = 1.5 * 2.0**23


def half_turn_fit():
    nodes = 0.125 * (1.0 - np.cos(np.pi * (np.arange(400) + 0.5) / 400))
    t = np.sqrt(nodes)
    root = math.sqrt(2.0)
    sin_c = np.polynomial.chebyshev.Chebyshev.fit(nodes, root * np.sin(np.pi * t) / t, 3, domain=[0, 0.25])
    cos_c = np.polynomial.chebyshev.Chebyshev.fit(nodes, root * np.cos(np.pi * t), 3, domain=[0, 0.25])
    to_list = lambda fit: [float(v) for v in fit.convert(kind=np.polynomial.Polynomial, domain=[-1, 1]).coef]
    return to_list(sin_c), to_list(cos_c)


SIN_C, COS_C = half_turn_fit()


def turn(spot):
    t = spot - ((spot + ROUND) - ROUND)
    u = t * t
    half_s = t * (((SIN_C[3] * u + SIN_C[2]) * u + SIN_C[1]) * u + SIN_C[0])
    half_c = ((COS_C[3] * u + COS_C[2]) * u + COS_C[1]) * u + COS_C[0]
    return (1.0 - half_s * half_s).astype(BF16), (half_s * half_c).astype(BF16)


def kernel(
    atoms, frac_hbm, feat_hbm, cot_hbm, kidx_hbm, smear_hbm, msg_ref, force_ref,
    frac_ref, feat_ref, cot_ref, kidx_ref, smear_ref, lsem,
    fr, f8, fs, xt, ph, gt, part, rc, s1, rx, s2, rz, fin,
    fsend, frecv, zsend, zrecv, xsend, xrecv, csend, crecv,
    pcs, pcr, pxs, pxr, pzs, pzr, ags, agr,
):
    bead = lax.axis_index("bead")
    z = lax.axis_index("atom")
    ka = lax.axis_index("ka")
    x = ka // 2
    core = lax.rem(ka, 2)
    slot = core * 2 + x
    other_core = 1 - core
    dev_z = [(bead, lax.rem(z + j, 4), ka) for j in range(4)]
    dev_core = (bead, z, x * 2 + other_core)
    dev_x = (bead, z, (1 - x) * 2 + core)
    dev_diag = (bead, z, (1 - x) * 2 + other_core)
    kn = kidx_ref.shape[1]
    quarter = fr.shape[2] // 4

    barrier = pltpu.get_barrier_semaphore()
    for dev in dev_z[1:] + [dev_core, dev_x, dev_diag]:
        pl.semaphore_signal(barrier, inc=1, device_id=dev, device_id_type=MESH)

    def remote(src, dst, send, recv, dev):
        return pltpu.make_async_remote_copy(
            src_ref=src, dst_ref=dst, send_sem=send, recv_sem=recv, device_id=dev, device_id_type=MESH
        )

    loads = [
        pltpu.make_async_copy(frac_hbm, frac_ref, lsem.at[0]),
        pltpu.make_async_copy(feat_hbm, feat_ref, lsem.at[1]),
        pltpu.make_async_copy(cot_hbm, cot_ref, lsem.at[2]),
        pltpu.make_async_copy(kidx_hbm.at[:, pl.ds(pl.multiple_of(z * kn, 128), kn)], kidx_ref, lsem.at[3]),
        pltpu.make_async_copy(smear_hbm, smear_ref, lsem.at[4]),
    ]
    for c in loads:
        c.start()
    f8[...] = jnp.zeros(f8.shape, F32)
    loads[0].wait()
    fr[0] = frac_ref[...]
    loads[1].wait()
    loads[2].wait()
    for s in range(4):
        cols = pl.ds(s * quarter, quarter)
        xt[0, s, 0:64, :] = feat_ref[:, cols]
        xt[0, s, 64:128, :] = cot_ref[:, cols]

    pl.semaphore_wait(barrier, 6)
    fcopies = [remote(fr.at[0], fr.at[4 - j], fsend.at[j], frecv.at[4 - j], dev_z[j]) for j in (1, 3, 2)]
    for c in fcopies:
        c.start()
    zcopies = [
        remote(xt.at[0, slot], xt.at[4 - j, slot], zsend.at[j], zrecv.at[4 - j], dev_z[j]) for j in (1, 3, 2)
    ]
    for c in zcopies:
        c.start()

    loads[3].wait()
    loads[4].wait()
    kf = kidx_ref[...].astype(F32)
    k0, k1, k2 = kf[0:1], kf[1:2], kf[2:3]
    row = lax.broadcasted_iota(jnp.int32, (8, kn), 0)
    k8 = jnp.where(row == 0, k0, jnp.where(row == 1, k1, jnp.where(row == 2, k2, 0.0)))
    kt = jnp.concatenate([k8, k8, k8, jnp.zeros((104, kn), F32)], axis=0).T.astype(BF16)[:, :32]

    def phases(r):
        f8[0:3, :] = fr[r]
        f = f8[...]
        hi = f.astype(BF16).astype(F32)
        mid = (f - hi).astype(BF16).astype(F32)
        lo = f - hi - mid
        fs[...] = jnp.concatenate([hi, mid, lo, jnp.zeros_like(f)], axis=0).astype(BF16)
        for s in range(4):
            spot = jnp.dot(kt, fs[:, s * quarter : (s + 1) * quarter], preferred_element_type=F32)
            c, sn = turn(spot)
            ph[r, s, 0:kn, :] = c
            ph[r, s, kn : 2 * kn, :] = sn

    def sums_of(r):
        waves = jnp.concatenate([ph[r, s] for s in range(4)], axis=1)
        both = jnp.concatenate([xt[r, s] for s in range(4)], axis=1)
        total = lax.dot_general(both, waves, (((1,), (1,)), ((), ())), preferred_element_type=F32)
        return total

    def wait_frac(r):
        remote(fr.at[0], fr.at[r], fsend.at[0], frecv.at[r], dev_x).wait_recv()

    nsq = k0 * k0 + k1 * k1 + k2 * k2
    srow = jnp.concatenate([smear_ref[...], smear_ref[...]], axis=1)
    scol = jnp.broadcast_to(srow, (128, 128)).T
    scol = jnp.concatenate([scol] * (kn // 128), axis=1)
    weights = jnp.exp(-scol * nsq) / (1.0 + nsq) * atoms ** (-0.5)
    mate = core * 2 + (1 - x)
    two = pl.ds(core * 2, 2)
    other_two = pl.ds(other_core * 2, 2)
    xcopies, ccopies = [], []

    def forward_x(r):
        remote(xt.at[0, slot], xt.at[r, slot], zsend.at[0], zrecv.at[r], dev_x).wait_recv()
        xcopies.append(remote(xt.at[r, slot], xt.at[r, slot], xsend.at[r], xrecv.at[r], dev_x))
        xcopies[-1].start()

    def forward_core(r):
        remote(xt.at[r, mate], xt.at[r, mate], xsend.at[r], xrecv.at[r], dev_x).wait_recv()
        ccopies.append(remote(xt.at[r, two], xt.at[r, two], csend.at[r], crecv.at[r], dev_core))
        ccopies[-1].start()

    def wait_core(r):
        remote(xt.at[r, other_two], xt.at[r, other_two], csend.at[r], crecv.at[r], dev_core).wait_recv()

    phases(0)
    wait_frac(1)
    phases(1)
    forward_x(1)
    total = sums_of(0)
    forward_x(3)
    wait_frac(3)
    phases(3)
    forward_core(1)
    forward_x(2)
    wait_frac(2)
    phases(2)
    forward_core(3)
    wait_core(1)
    total = total + sums_of(1)
    forward_core(2)
    wait_core(3)
    total = total + sums_of(3)
    wait_core(2)
    total = total + sums_of(2)
    sums_t = total

    wc = (sums_t[:, :kn] * weights).astype(BF16)
    ws = (sums_t[:, kn:] * weights).astype(BF16)
    half = wc.shape[0] // 2
    gt[384:448, 0:kn] = wc[:half]
    gt[384:448, kn : 2 * kn] = ws[:half]
    wc, ws = wc.astype(F32), ws.astype(F32)
    wc = jnp.concatenate([wc[half:], wc[:half]], axis=0)
    ws = jnp.concatenate([ws[half:], ws[:half]], axis=0)
    for d, kd in enumerate((k0, k1, k2)):
        gt[128 * d : 128 * d + 128, 0:kn] = (ws * kd).astype(BF16)
        gt[128 * d : 128 * d + 128, kn : 2 * kn] = (wc * -kd).astype(BF16)

    frow = lax.broadcasted_iota(jnp.int32, (16, quarter), 0)

    def outputs_of(r, i, slots):
        for s in slots:
            out = jnp.dot(gt[...], ph[r, s], preferred_element_type=F32)
            pair = xt[r, s].astype(F32)
            f = [
                -TWO_PI * jnp.sum(out[128 * d : 128 * d + 128] * pair, axis=0, keepdims=True) for d in range(3)
            ]
            part[i, s, 0:64, :] = out[384:448].astype(BF16)
            part[i, s, 64:80, :] = jnp.where(
                frow == 0, f[0], jnp.where(frow == 1, f[1], jnp.where(frow == 2, f[2], 0.0))
            ).astype(BF16)

    pending = []

    def begin(c):
        c.start()
        pending.append(c)

    def to_core(i):
        outputs_of((1 + i) % 4, i, (other_core * 2, other_core * 2 + 1))
        begin(remote(part.at[i, other_two], rc.at[i], pcs.at[i], pcr.at[i], dev_core))

    def to_x(i):
        outputs_of((1 + i) % 4, i, (mate,))
        remote(part.at[i, two], rc.at[i], pcs.at[i], pcr.at[i], dev_core).wait_recv()
        s1[i] = (part[i, mate].astype(F32) + rc[i, 1 - x].astype(F32)).astype(BF16)
        begin(remote(s1.at[i], rx.at[i], pxs.at[i], pxr.at[i], dev_x))

    to_core(0)
    for i in range(1, 4):
        to_core(i)
        to_x(i - 1)
    to_x(3)
    own = None
    for i in range(4):
        outputs_of((1 + i) % 4, i, (slot,))
        remote(s1.at[i], rx.at[i], pxs.at[i], pxr.at[i], dev_x).wait_recv()
        own = part[i, slot].astype(F32) + rc[i, x].astype(F32) + rx[i].astype(F32)
        if i < 3:
            s2[i] = own.astype(BF16)
            begin(remote(s2.at[i], rz.at[i], pzs.at[i], pzr.at[i], dev_z[1 + i]))
    for j in range(3):
        remote(s2.at[j], rz.at[j], pzs.at[j], pzr.at[j], dev_x).wait_recv()
        own = own + rz[j].astype(F32)
    fin[slot] = own.astype(BF16)
    for j, dev in enumerate((dev_x, dev_core, dev_diag)):
        begin(remote(fin.at[slot], fin.at[slot], ags.at[j], agr.at[j], dev))
    slots = (mate, other_core * 2 + x, other_core * 2 + (1 - x))
    for j, dev in enumerate((dev_x, dev_core, dev_diag)):
        remote(fin.at[slots[j]], fin.at[slots[j]], ags.at[j], agr.at[j], dev).wait_recv()
    for s in range(4):
        msg_ref[:, s * quarter : (s + 1) * quarter] = fin[s, 0:64, :].astype(F32)
        force_ref[:, s * quarter : (s + 1) * quarter] = fin[s, 64:80, :].astype(F32)[0:3]
    for c in fcopies + zcopies + xcopies + ccopies + pending:
        c.wait_send()


def fast_on_device(frac, feat, cotan, kidx, smear):
    rows, chans = feat.shape
    kn = kidx.shape[1] // 4
    quarter = rows // 4
    dma = pltpu.SemaphoreType.DMA
    vmem = pl.BlockSpec(memory_space=pltpu.VMEM)
    messages_t, forces = pl.pallas_call(
        functools.partial(kernel, 4 * rows),
        out_shape=(jax.ShapeDtypeStruct((chans, rows), F32), jax.ShapeDtypeStruct((3, rows), F32)),
        in_specs=[pl.BlockSpec(memory_space=pl.ANY)] * 5,
        out_specs=(vmem, vmem),
        scratch_shapes=[
            pltpu.VMEM((3, rows), F32),
            pltpu.VMEM((chans, rows), BF16),
            pltpu.VMEM((chans, rows), BF16),
            pltpu.VMEM((3, kn), jnp.int32),
            pltpu.VMEM((1, chans), F32),
            dma((5,)),
            pltpu.VMEM((4, 3, rows), F32),
            pltpu.VMEM((8, rows), F32),
            pltpu.VMEM((32, rows), BF16),
            pltpu.VMEM((4, 4, 128, quarter), BF16),
            pltpu.VMEM((4, 4, 2 * kn, quarter), BF16),
            pltpu.VMEM((448, 2 * kn), BF16),
            pltpu.VMEM((4, 4, 80, quarter), BF16),
            pltpu.VMEM((4, 2, 80, quarter), BF16),
            pltpu.VMEM((4, 80, quarter), BF16),
            pltpu.VMEM((4, 80, quarter), BF16),
            pltpu.VMEM((3, 80, quarter), BF16),
            pltpu.VMEM((3, 80, quarter), BF16),
            pltpu.VMEM((4, 80, quarter), BF16),
        ]
        + [dma((4,))] * 16,
        compiler_params=pltpu.CompilerParams(
            collective_id=0, has_side_effects=True, vmem_limit_bytes=48 * 1024 * 1024
        ),
    )(frac, feat.T, cotan.T, kidx, smear.reshape(1, chans))
    return messages_t.T, forces


def over_rows(table, columns):
    return lax.dot_general(table, columns, (((0,), (0,)), ((), ())), preferred_element_type=F32)


def plain_on_device(frac, feat, cotan, kidx, smear):
    rows, chans = feat.shape
    atoms = rows * lax.axis_size("atom")
    nf = kidx.astype(F32)
    nsq = nf[0] * nf[0] + nf[1] * nf[1] + nf[2] * nf[2]
    weights = jnp.exp(-smear[None, :] * nsq[:, None]) / (1.0 + nsq)[:, None] * atoms ** (-0.5)
    spot = frac[0][:, None] * nf[0][None, :] + frac[1][:, None] * nf[1][None, :]
    cos_t, sin_t = turn(spot + frac[2][:, None] * nf[2][None, :])
    both = jnp.concatenate([feat, cotan], axis=1)
    sums = jnp.concatenate([over_rows(cos_t, both), over_rows(sin_t, both)], axis=1)
    total = lax.psum(sums, "atom")
    weighted = (total * jnp.tile(weights, (1, 4))).astype(BF16)
    left_c, left_s = weighted[:, : 2 * chans], weighted[:, 2 * chans :]
    msg = jnp.dot(cos_t, left_c[:, :chans], preferred_element_type=F32)
    msg = msg + jnp.dot(sin_t, left_s[:, :chans], preferred_element_type=F32)
    pair = jnp.concatenate([cotan, feat], axis=1)
    against = lambda a, b: lax.dot_general(a, b, (((1,), (1,)), ((), ())), preferred_element_type=F32)
    p_part, q_part = against(pair, left_c), against(pair, left_s)
    slope = (cos_t.astype(F32) * q_part - sin_t.astype(F32) * p_part).astype(BF16)
    force = -TWO_PI * against(kidx.astype(BF16), slope)
    return lax.psum(msg, "ka"), lax.psum(force, "ka")


def on_device(frac, feat, cotan, kidx, smear):
    rows, chans = feat.shape
    fits = lax.axis_size("atom") == 4 and lax.axis_size("ka") == 4 and chans == 64
    fits = fits and rows % 512 == 0 and rows <= 1024 and kidx.shape[1] % 512 == 0 and kidx.shape[1] <= 2048
    return (fast_on_device if fits else plain_on_device)(frac, feat, cotan, kidx, smear)


def solution(mesh):
    return jax.shard_map(
        on_device,
        mesh=mesh,
        in_specs=(
            P(None, ("bead", "atom")),
            P(("bead", "atom"), None),
            P(("bead", "atom"), None),
            P(None, "ka"),
            P(),
        ),
        out_specs=(P(("bead", "atom"), None), P(None, ("bead", "atom"))),
        check_vma=False,
    )
```
